32 devices in a mesh: groups: 2 (over x), dp: 8 (over z, y), tensor: 2 (over core).
Axes of the slice: x: 2, y: 2, z: 4, core: 2. Of those that a mesh axis runs over, the one named last changes fastest.
Arguments:
- hidden_states: bfloat16 [3584, 5120], P(('groups', 'dp'), 'tensor'), parts along dimension 0, may hold values from -6 to 6
- input_gain: float32 [5120], replicated, may hold values from 0.1 to 1.9
- q_weight: bfloat16 [5120, 512], P(None, 'tensor'), may hold values from -0.078125 to 0.078125
- k_weight: bfloat16 [5120, 256], P(None, 'tensor'), may hold values from -0.078125 to 0.078125
- v_weight: bfloat16 [5120, 256], P(None, 'tensor'), may hold values from -0.078125 to 0.078125
- o_weight: bfloat16 [512, 5120], P('tensor'), may hold values from -0.25 to 0.25
- q_gain: float32 [128], replicated, may hold values from 0.6 to 13
- k_gain: float32 [128], replicated, may hold values from 0.6 to 13
- seq_lens: int32 [16, 5], P('groups'), parts along dimension 0, may hold values from 1 to 160, as said below
- dest: int32 [16, 5], P('groups'), parts along dimension 0, may hold values from 0 to 7, as said below
Outputs:
- mixed: bfloat16 [2560, 5120], P(('groups', 'dp'), 'tensor'), parts along dimension 0
The draws below stay inside these ranges and needn't reach their ends.
There are 2 independent parts, one for each index of `groups`. The reference program is written for one: setup_inputs(seed, part) draws one part's arguments, and reference() takes and returns one part's arrays. A program takes and returns all parts, laid end to end along the dimension named above; an argument that names none is the same for every part. Nothing has to cross between parts.
Inputs may be any that keep to these rules, and one draw needn't show every extreme that they name: `seq_lens`: each replica's sequences lie packed from row 0 of its block in slot order. `dest`: slot 0 never moves. A replica either sends sequences or receives them, never both. At most 16 tokens in all go from one replica to any one other, and at most 160 tokens are processed by one replica; both bounds are reached.
All inputs are finite; a program needn't handle non-finite values.
Results may differ from the reference program's by a relative error of at most 0.004.
The reference program's roundings to bfloat16 on the way count: a program that leaves them out, or rounds other values in their place, can miss the bound.
Values may be sent and summed in bfloat16 or wider, within the bound.
A program may use at most 128 MiB of HBM per device.

```python
import jax
import jax.numpy as jnp
from jax import lax

D = 5120
HD = 128
KV = 2
QPK = 2
CAPP = 16
LONG = 160
SHORT = 8
NSEQ = 5
HOME = 224
WORK = 160
N_DP = 8


def replica_roles(key):
    shuffled = jax.random.permutation(jax.random.fold_in(key, 101), N_DP).astype(jnp.int32)
    standing = jnp.argsort(shuffled).astype(jnp.int32)
    return (shuffled, standing)


def head_gain(key):
    base = jax.random.uniform(key, (HD,), jnp.float32, 0.6, 1.6)
    channel = jnp.arange(HD) % (HD // 2)
    slow = channel >= HD // 2 - max(HD // 16, 1)
    return jnp.where(slow, base, base)


def draw_seq_lens(key, part):
    shuffled, standing = replica_roles(key)
    key = jax.random.fold_in(key, 1)
    half_count = N_DP // 2
    slot_index = jnp.arange(NSEQ, dtype=jnp.int32)[None, :]
    sender = (standing < half_count)[:, None]
    long_len = jax.random.randint(jax.random.fold_in(key, 2), (N_DP, 1), LONG // 2, LONG + 1)
    long_len = jnp.where((standing == 0)[:, None], LONG, long_len)
    ship_len = jax.random.randint(jax.random.fold_in(key, 3), (N_DP, NSEQ), CAPP - CAPP // 4, CAPP + 1)
    ship_len = jnp.where((standing[:, None] + slot_index) % half_count == 0, CAPP, ship_len)
    own_len = jax.random.randint(jax.random.fold_in(key, 4), (N_DP, NSEQ), 1, SHORT + 1)
    own_len = jnp.where((standing == half_count)[:, None], SHORT, own_len)
    heavy_len = jnp.where(slot_index == 0, long_len, ship_len)
    return jnp.where(sender, heavy_len, own_len).astype(jnp.int32)


def draw_dest(key, part):
    shuffled, standing = replica_roles(key)
    half_count = N_DP // 2
    slot_index = jnp.arange(NSEQ, dtype=jnp.int32)[None, :]
    receiver = jnp.take(shuffled, half_count + (standing[:, None] + slot_index) % half_count)
    own_replica = jnp.arange(N_DP, dtype=jnp.int32)[:, None]
    moving = (standing[:, None] < half_count) & (slot_index > 0)
    return jnp.where(moving, receiver, own_replica).astype(jnp.int32)


def draw_q_gain(key, part):
    key = jax.random.fold_in(key, 11)
    return head_gain(key)


def draw_k_gain(key, part):
    key = jax.random.fold_in(key, 13)
    return head_gain(key)


def level_of(own_key, extent, pieces, least, top_value):
    level = 1.0
    for dim, blocks in pieces:
        heights = jax.random.uniform(jax.random.fold_in(jax.random.fold_in(own_key, 6), dim), (blocks,), jnp.float32, least / len(pieces), top_value / len(pieces))
        level = level * jnp.repeat(jnp.exp(heights), extent[dim] // blocks).reshape((-1,) + (1,) * (len(extent) - 1 - dim))
    return level


def bell_draw(key, shape, deviation, limit, shards=(), held_as=jnp.bfloat16):
    level = level_of(key, shape, shards, -0.22, 0.18) if shards else 1.0
    values = jax.random.normal(key, shape, jnp.float32) * deviation * level
    return jnp.minimum(jnp.maximum(values, -limit), limit).astype(held_as)


def setup_inputs(seed: int = 0, part: int = 0) -> dict:
    streams_of = jax.random.split(jax.random.key(seed), 11)
    own_keys = jax.random.split(jax.random.fold_in(streams_of[10], part), 11)
    return {
        "hidden_states": bell_draw(own_keys[0], (N_DP * HOME, D), 1.0, 6.0, ((0, 8), (1, 2))),
        "input_gain": jnp.clip(1.0 + 0.18 * jax.random.normal(streams_of[1], (D,), jnp.float32), 0.1, 1.9),
        "q_weight": bell_draw(streams_of[2], (D, KV * QPK * HD), D ** -0.5, 0.078125, ((1, 2),)),
        "k_weight": bell_draw(streams_of[3], (D, KV * HD), D ** -0.5, 0.078125, ((1, 2),)),
        "v_weight": bell_draw(streams_of[4], (D, KV * HD), D ** -0.5, 0.078125, ((1, 2),)),
        "o_weight": bell_draw(streams_of[5], (KV * QPK * HD, D), (KV * QPK * HD) ** -0.5, 0.25, ((0, 2),)),
        "q_gain": draw_q_gain(jax.random.fold_in(streams_of[10], 71), part),
        "k_gain": draw_k_gain(jax.random.fold_in(streams_of[10], 71), part),
        "seq_lens": draw_seq_lens(jax.random.fold_in(jax.random.fold_in(streams_of[10], part), 71), part),
        "dest": draw_dest(jax.random.fold_in(jax.random.fold_in(streams_of[10], part), 71), part),
    }


EPSILON = 1e-06
ROPE_BASE = 1000000.0
MASKED_SCORE = -1e+30

def rms_scale(entries, gain):
    mean_square = lax.optimization_barrier(jnp.mean(entries * entries, axis=-1, keepdims=True))
    return entries * lax.rsqrt(mean_square + EPSILON) * gain

def rotation(positions, width):
    half_head = width // 2
    frequency = ROPE_BASE ** (-2.0 * jnp.arange(half_head, dtype=jnp.float32) / width)
    angles = positions.astype(jnp.float32)[:, None] * frequency[None, :]
    return (jnp.cos(angles), jnp.sin(angles))

def rotate(entries, cosine, sine_part):
    half_head = entries.shape[-1] // 2
    first_half = entries[..., :half_head]
    second_half = entries[..., half_head:]
    return jnp.concatenate([first_half * cosine - second_half * sine_part, second_half * cosine + first_half * sine_part], axis=-1)

def sequence_table(seq_lens, dest):
    replicas, slots = seq_lens.shape
    lengths = seq_lens.reshape(-1).astype(jnp.int32)
    offsets = (jnp.cumsum(seq_lens, axis=1) - seq_lens).reshape(-1).astype(jnp.int32)
    source = jnp.broadcast_to(jnp.arange(replicas, dtype=jnp.int32)[:, None], (replicas, slots)).reshape(-1)
    slot_index = jnp.broadcast_to(jnp.arange(slots, dtype=jnp.int32)[None, :], (replicas, slots)).reshape(-1)
    target = dest.reshape(-1).astype(jnp.int32)
    order_key = (source - target) % replicas * slots + slot_index
    earlier = (target[None, :] == target[:, None]) & (order_key[None, :] < order_key[:, None])
    begins = lax.optimization_barrier(jnp.sum(jnp.where(earlier, lengths[None, :], 0), axis=1)).astype(jnp.int32)
    return (source, slot_index, lengths, target, offsets, begins)

def reference(hidden_states, input_gain, q_weight, k_weight, v_weight, o_weight, q_gain, k_gain, seq_lens, dest):
    source, slot_index, lengths, target, offsets, begins = sequence_table(seq_lens, dest)
    seq_ident = jnp.arange(lengths.shape[0], dtype=jnp.int32)
    head_total = KV * QPK

    def one_replica(replica):
        row_ids = jnp.arange(WORK, dtype=jnp.int32)[:, None]
        placed = (target[None, :] == replica) & (begins[None, :] <= row_ids) & (row_ids < begins[None, :] + lengths[None, :])
        live_row = jnp.any(placed, axis=1)
        position = lax.optimization_barrier(jnp.sum(jnp.where(placed, row_ids - begins[None, :], 0), axis=1)).astype(jnp.int32)
        sequence = jnp.where(live_row, lax.optimization_barrier(jnp.sum(jnp.where(placed, seq_ident[None, :], 0), axis=1)), -1).astype(jnp.int32)
        home_row = (lax.optimization_barrier(jnp.sum(jnp.where(placed, source[None, :] * HOME + offsets[None, :], 0), axis=1)) + position).astype(jnp.int32)
        gathered = jnp.take(hidden_states, home_row, axis=0)
        wide_rows = gathered.astype(jnp.float32)
        normed = rms_scale(wide_rows, input_gain).astype(jnp.bfloat16)
        cosine, sine_part = rotation(position, HD)
        queries = jnp.dot(normed, q_weight, preferred_element_type=jnp.float32).reshape(WORK, head_total, HD)
        queries = rotate(rms_scale(queries, q_gain), cosine[:, None, :], sine_part[:, None, :]).astype(jnp.bfloat16)
        key_rows = jnp.dot(normed, k_weight, preferred_element_type=jnp.float32).reshape(WORK, KV, HD)
        key_rows = rotate(rms_scale(key_rows, k_gain), cosine[:, None, :], sine_part[:, None, :]).astype(jnp.bfloat16)
        value_rows = jnp.dot(normed, v_weight, preferred_element_type=jnp.float32).astype(jnp.bfloat16).reshape(WORK, KV, HD)
        key_rows = jnp.repeat(key_rows, QPK, axis=1)
        value_rows = jnp.repeat(value_rows, QPK, axis=1)
        scores = jnp.einsum('qhd,khd->hqk', queries.astype(jnp.float32), key_rows.astype(jnp.float32)) * HD ** (-0.5)
        allowed = (sequence[:, None] == sequence[None, :]) & (position[None, :] <= position[:, None])
        scores = jnp.where(allowed[None], scores, MASKED_SCORE)
        row_max = lax.optimization_barrier(jnp.max(scores, axis=2, keepdims=True))
        exp_scores = jnp.exp(scores - row_max)
        weights = (exp_scores / lax.optimization_barrier(jnp.sum(exp_scores, axis=2, keepdims=True))).astype(jnp.bfloat16)
        head_out = jnp.einsum('hqk,khd->qhd', weights.astype(jnp.float32), value_rows.astype(jnp.float32))
        head_out = head_out.astype(jnp.bfloat16).reshape(WORK, head_total * HD)
        attention = jnp.dot(head_out, o_weight, preferred_element_type=jnp.float32)
        return jnp.where(live_row[:, None], wide_rows + attention, 0.0).astype(jnp.bfloat16)
    blocks = lax.map(one_replica, jnp.arange(N_DP, dtype=jnp.int32))
    return blocks.reshape(N_DP * WORK, D)
```

```python
import functools

import jax
import jax.numpy as jnp
import numpy as np
from jax import lax
from jax.experimental import pallas as pl
from jax.experimental.pallas import tpu as pltpu
from jax.sharding import PartitionSpec as P

HD = 128
CAPP = 16
LONG = 160
SHORT = 8
CHUNK = 512

EPSILON = 1e-06
ROPE_BASE = 1000000.0
MASKED_SCORE = -1e30
MESH = pl.DeviceIdType.MESH
F32 = jnp.float32
BF16 = jnp.bfloat16


def one_hot(hit):
    return jnp.where(hit, 1.0, 0.0).astype(BF16)


def dot(a, b):
    return jnp.dot(a, b, preferred_element_type=F32)


def head_norm(entries, gain):
    mean_square = jnp.mean(entries * entries, axis=-1, keepdims=True)
    return entries * lax.rsqrt(mean_square + EPSILON) * gain


def kernel(
    replicas,
    lens_ref,
    dest_ref,
    rope_ref,
    q_gain_ref,
    k_gain_ref,
    gain_ref,
    x_hbm,
    qw_hbm,
    kw_hbm,
    vw_hbm,
    o_hbm,
    out_hbm,
    x_own,
    x_other,
    w_all,
    o_all,
    x_send,
    x_recv,
    h_own,
    h_other,
    h_send,
    h_recv,
    qkv,
    out_buf,
    load_sem,
    pair_send,
    pair_recv,
    xs_sem,
    xr_sem,
    hs_sem,
    hr_sem,
    out_sem,
):
    me = lax.axis_index("dp")
    part = lax.axis_index("tensor")
    home, half = x_own.shape
    work = out_buf.shape[0]
    slots = lens_ref.shape[1]
    chunks = half // CHUNK
    peers = [lax.rem(me + k, replicas) for k in range(replicas)]

    barrier = pltpu.get_barrier_semaphore()
    for k in range(1, replicas):
        pl.semaphore_signal(barrier, inc=1, device_id={"dp": peers[k]}, device_id_type=MESH)
    pl.semaphore_signal(barrier, inc=1, device_id={"tensor": 1 - part}, device_id_type=MESH)

    own_cols = pl.ds(pl.multiple_of(part * half, CHUNK), half)
    other_cols = pl.ds(pl.multiple_of((1 - part) * half, CHUNK), half)
    loads = [
        pltpu.make_async_copy(x_hbm, x_own, load_sem.at[0]),
        pltpu.make_async_copy(qw_hbm, w_all.at[:, pl.ds(0, 2 * HD)], load_sem.at[1]),
        pltpu.make_async_copy(kw_hbm, w_all.at[:, pl.ds(2 * HD, HD)], load_sem.at[2]),
        pltpu.make_async_copy(vw_hbm, w_all.at[:, pl.ds(3 * HD, HD)], load_sem.at[3]),
        pltpu.make_async_copy(o_hbm.at[:, own_cols], o_all.at[0], load_sem.at[4]),
    ]
    for load in loads:
        load.start()

    lens = [lens_ref[me, s] for s in range(slots)]
    dests = [dest_ref[me, s] for s in range(slots)]
    row = lax.broadcasted_iota(jnp.int32, (1, home), 1)
    col = lax.broadcasted_iota(jnp.int32, (home, 1), 0)
    to_send = jnp.full((1, home), -1, jnp.int32)
    to_work = jnp.full((1, home), -1, jnp.int32)
    start = jnp.zeros((home, 1), jnp.int32)
    offset = jnp.int32(0)
    staying = jnp.int32(0)
    for s in range(slots):
        before = jnp.int32(0)
        for t in range(s):
            before = before + jnp.where(dests[t] == dests[s], lens[t], 0)
        shift = dests[s] - me
        shift = jnp.where(shift < 0, shift + replicas, shift)
        stays = shift == 0
        send_base = jnp.where(stays, -home, shift * CAPP + before - offset)
        work_base = jnp.where(stays, before - offset, -2 * home)
        to_send = jnp.where(row >= offset, row + send_base - jnp.where(stays, home, 0), to_send)
        to_work = jnp.where(row >= offset, row + work_base, to_work)
        start = jnp.where(col >= offset, offset, start)
        staying = staying + jnp.where(stays, lens[s], 0)
        offset = offset + lens[s]
    to_send = jnp.where(row >= offset, -1, to_send)
    to_work = jnp.where(row >= offset, -1, to_work)
    pool = replicas * CAPP
    send_hot = one_hot(lax.broadcasted_iota(jnp.int32, (pool, home), 0) == to_send)

    x_recv[pl.ds(0, CAPP), :] = jnp.zeros((CAPP, half), BF16)
    h_recv[pl.ds(0, CAPP), :] = jnp.zeros((CAPP, h_recv.shape[1]), BF16)

    loads[0].wait()

    @pl.loop(0, chunks)
    def _(c):
        cols = pl.ds(pl.multiple_of(c * CHUNK, CHUNK), CHUNK)
        x_send[:, cols] = dot(send_hot, x_own[:, cols]).astype(BF16)

    pl.semaphore_wait(barrier, replicas)

    pair_x = pltpu.make_async_remote_copy(
        x_own, x_other, pair_send.at[0], pair_recv.at[0], {"tensor": 1 - part}, MESH
    )
    pair_x.start()

    def exchange(source, target, send_sem, recv_sem):
        copies = []
        for k in range(1, replicas):
            copies.append(
                pltpu.make_async_remote_copy(
                    source.at[pl.ds(k * CAPP, CAPP)],
                    target.at[pl.ds((replicas - k) * CAPP, CAPP)],
                    send_sem.at[k],
                    recv_sem.at[replicas - k],
                    {"dp": peers[k]},
                    MESH,
                )
            )
        for copy in copies:
            copy.start()
        return copies

    x_copies = exchange(x_send, x_recv, xs_sem, xr_sem)
    pair_o = pltpu.make_async_remote_copy(
        o_hbm.at[:, other_cols], o_all.at[1], pair_send.at[1], pair_recv.at[1], {"tensor": 1 - part}, MESH
    )
    pair_o.start()

    slot = lax.broadcasted_iota(jnp.int32, (1, pool), 1)
    from_pool = jnp.full((1, pool), -1, jnp.int32)
    begin = staying
    for k in range(1, replicas):
        count = jnp.int32(0)
        for s in range(slots):
            count = count + jnp.where(dest_ref[peers[k], s] == me, lens_ref[peers[k], s], 0)
        inside = (slot >= k * CAPP) & (slot < k * CAPP + count)
        from_pool = jnp.where(inside, slot + (begin - k * CAPP), from_pool)
        begin = begin + count
    home_hot = one_hot(lax.broadcasted_iota(jnp.int32, (work, home), 0) == to_work)
    pool_hot = one_hot(lax.broadcasted_iota(jnp.int32, (work, pool), 0) == from_pool)

    angles = (col - start).astype(F32) * rope_ref[0:1, :]
    cosine = jnp.cos(angles)
    sine = jnp.sin(angles) * rope_ref[1:2, :]

    def square_sum(x_ref):
        def step(c, total):
            for piece in range(CHUNK // 128):
                cols = pl.ds(pl.multiple_of(c * CHUNK + piece * 128, 128), 128)
                wide = x_ref[:, cols].astype(F32)
                total = total + wide * wide
            return total

        return lax.fori_loop(0, chunks, step, jnp.zeros((home, 128), F32))

    own_squares = square_sum(x_own)
    pair_x.wait_recv()
    squares = own_squares + square_sum(x_other)
    scale = lax.rsqrt(jnp.sum(squares, axis=1, keepdims=True) / (2 * half) + EPSILON)
    for load in loads[1:4]:
        load.wait()
    qkv[...] = jnp.zeros_like(qkv)
    for x_ref, base in ((x_own, part * half), (x_other, (1 - part) * half)):

        @pl.loop(0, chunks)
        def _(c, x_ref=x_ref, base=base):
            cols = pl.ds(pl.multiple_of(c * CHUNK, CHUNK), CHUNK)
            rows = pl.ds(pl.multiple_of(base + c * CHUNK, CHUNK), CHUNK)
            normed = (x_ref[:, cols].astype(F32) * scale * gain_ref[:, rows]).astype(BF16)
            qkv[...] += dot(normed, w_all[rows, :])

    def rotated(entries, gain):
        entries = head_norm(entries, gain)
        return (entries * cosine + pltpu.roll(entries, HD // 2, 1) * sine).astype(BF16)

    keys = rotated(qkv[:, pl.ds(2 * HD, HD)], k_gain_ref[...])
    values = qkv[:, pl.ds(3 * HD, HD)].astype(BF16)
    key_id = lax.broadcasted_iota(jnp.int32, (home, home), 1)
    query_id = lax.broadcasted_iota(jnp.int32, (home, home), 0)
    allowed = (key_id >= start) & (key_id <= query_id)
    for h in range(2):
        queries = rotated(qkv[:, pl.ds(h * HD, HD)], q_gain_ref[...])
        scores = lax.dot_general(
            queries, keys, (((1,), (1,)), ((), ())), preferred_element_type=F32
        ) * HD ** (-0.5)
        scores = jnp.where(allowed, scores, MASKED_SCORE)
        exp_scores = jnp.exp(scores - jnp.max(scores, axis=1, keepdims=True))
        weights = (exp_scores / jnp.sum(exp_scores, axis=1, keepdims=True)).astype(BF16)
        h_own[:, pl.ds(h * HD, HD)] = dot(weights, values).astype(BF16)

    pair_h = pltpu.make_async_remote_copy(
        h_own, h_other, pair_send.at[2], pair_recv.at[2], {"tensor": 1 - part}, MESH
    )
    pair_h.start()
    width = h_own.shape[1]
    h_send[:, pl.ds(0, width)] = dot(send_hot, h_own[...]).astype(BF16)
    pair_h.wait_recv()
    h_send[:, pl.ds(width, width)] = dot(send_hot, h_other[...]).astype(BF16)
    h_copies = exchange(h_send, h_recv, hs_sem, hr_sem)

    home_own = dot(home_hot, h_own[...])
    home_other = dot(home_hot, h_other[...])
    for copy in x_copies:
        copy.wait_recv()
    for copy in h_copies:
        copy.wait_recv()
    loads[4].wait()
    pair_o.wait_recv()
    all_own = (home_own + dot(pool_hot, h_recv[:, pl.ds(0, width)])).astype(BF16)
    all_other = (home_other + dot(pool_hot, h_recv[:, pl.ds(width, width)])).astype(BF16)

    @pl.loop(0, chunks)
    def _(c):
        cols = pl.ds(pl.multiple_of(c * CHUNK, CHUNK), CHUNK)
        moved = dot(home_hot, x_own[:, cols]) + dot(pool_hot, x_recv[:, cols])
        attended = dot(all_own, o_all[0, :, cols]) + dot(all_other, o_all[1, :, cols])
        out_buf[:, cols] = (moved + attended).astype(BF16)

    result = pltpu.make_async_copy(out_buf, out_hbm, out_sem)
    result.start()
    for copy in [pair_x, pair_o, pair_h] + x_copies + h_copies:
        copy.wait_send()
    result.wait()


def per_device(
    hidden_states,
    input_gain,
    q_weight,
    k_weight,
    v_weight,
    o_weight,
    q_gain,
    k_gain,
    seq_lens,
    dest,
):
    replicas = lax.axis_size("dp")
    home, half = hidden_states.shape
    slots = seq_lens.shape[1]
    work = max(LONG, slots * SHORT + (slots - 1) * CAPP)
    pool = replicas * CAPP
    width = o_weight.shape[0]
    channel = np.arange(HD)
    frequency = ROPE_BASE ** (-2.0 * (channel % (HD // 2)) / HD)
    sign = np.where(channel < HD // 2, -1.0, 1.0)
    rope = jnp.asarray(np.stack([frequency, sign]).astype(np.float32))
    vmem = pl.BlockSpec(memory_space=pltpu.VMEM)
    smem = pl.BlockSpec(memory_space=pltpu.SMEM)
    hbm = pl.BlockSpec(memory_space=pl.ANY)
    dma = pltpu.SemaphoreType.DMA
    return pl.pallas_call(
        functools.partial(kernel, replicas),
        out_shape=jax.ShapeDtypeStruct((work, half), BF16),
        in_specs=[smem, smem, vmem, vmem, vmem, vmem] + [hbm] * 5,
        out_specs=hbm,
        scratch_shapes=[
            pltpu.VMEM((home, half), BF16),
            pltpu.VMEM((home, half), BF16),
            pltpu.VMEM((2 * half, 4 * HD), BF16),
            pltpu.VMEM((2, width, half), BF16),
            pltpu.VMEM((pool, half), BF16),
            pltpu.VMEM((pool, half), BF16),
            pltpu.VMEM((home, width), BF16),
            pltpu.VMEM((home, width), BF16),
            pltpu.VMEM((pool, 2 * width), BF16),
            pltpu.VMEM((pool, 2 * width), BF16),
            pltpu.VMEM((home, 4 * HD), F32),
            pltpu.VMEM((work, half), BF16),
            dma((5,)),
            dma((3,)),
            dma((3,)),
            dma((replicas,)),
            dma((replicas,)),
            dma((replicas,)),
            dma((replicas,)),
            dma,
        ],
        compiler_params=pltpu.CompilerParams(
            collective_id=0,
            has_side_effects=True,
            vmem_limit_bytes=56 * 1024 * 1024,
        ),
    )(
        seq_lens,
        dest,
        rope,
        q_gain.reshape(1, HD),
        k_gain.reshape(1, HD),
        input_gain.reshape(1, -1),
        hidden_states,
        q_weight,
        k_weight,
        v_weight,
        o_weight,
    )


def solution(mesh):
    return jax.shard_map(
        per_device,
        mesh=mesh,
        in_specs=(
            P(("groups", "dp"), "tensor"),
            P(),
            P(None, "tensor"),
            P(None, "tensor"),
            P(None, "tensor"),
            P("tensor", None),
            P(),
            P(),
            P("groups", None),
            P("groups", None),
        ),
        out_specs=P(("groups", "dp"), "tensor"),
        check_vma=False,
    )
```

```python
import functools

import jax
import jax.numpy as jnp
import numpy as np
from jax import lax
from jax.experimental import pallas as pl
from jax.experimental.pallas import tpu as pltpu
from jax.sharding import PartitionSpec as P

HD = 128
CAPP = 16
LONG = 160
SHORT = 8
CHUNK = 512
WIDE = 1280

EPSILON = 1e-06
ROPE_BASE = 1000000.0
MASKED_SCORE = -1e30
MESH = pl.DeviceIdType.MESH
F32 = jnp.float32
BF16 = jnp.bfloat16


def one_hot(hit):
    return jnp.where(hit, 1.0, 0.0).astype(BF16)


def dot(a, b):
    return jnp.dot(a, b, preferred_element_type=F32)


def head_norm(entries, gain):
    mean_square = jnp.mean(entries * entries, axis=-1, keepdims=True)
    return entries * lax.rsqrt(mean_square + EPSILON) * gain


def kernel(
    replicas,
    lens_ref,
    dest_ref,
    rope_ref,
    q_gain_ref,
    k_gain_ref,
    gain_ref,
    x_hbm,
    qw_hbm,
    kw_hbm,
    vw_hbm,
    o_hbm,
    out_hbm,
    x_own,
    x_other,
    w_all,
    o_all,
    x_send,
    x_recv,
    h_own,
    h_other,
    h_send,
    h_recv,
    h_pass,
    squares_own,
    squares_other,
    qkv,
    result,
    out_buf,
    load_sem,
    pair_send,
    pair_recv,
    xs_sem,
    xr_sem,
    hs_sem,
    hr_sem,
    out_sem,
):
    me = lax.axis_index("dp")
    part = lax.axis_index("tensor")
    home, half = x_own.shape
    work = out_buf.shape[0]
    slots = lens_ref.shape[1]
    chunks = half // CHUNK
    ahead = chunks * 2 // 5
    early = pl.ds(0, ahead * CHUNK)
    late = pl.ds(ahead * CHUNK, half - ahead * CHUNK)
    peers = [lax.rem(me + k, replicas) for k in range(replicas)]

    barrier = pltpu.get_barrier_semaphore()
    for k in range(1, replicas):
        pl.semaphore_signal(barrier, inc=1, device_id={"dp": peers[k]}, device_id_type=MESH)
    pl.semaphore_signal(barrier, inc=1, device_id={"tensor": 1 - part}, device_id_type=MESH)

    own_cols = pl.ds(pl.multiple_of(part * half, CHUNK), half)
    other_cols = pl.ds(pl.multiple_of((1 - part) * half, CHUNK), half)
    loads = [
        pltpu.make_async_copy(x_hbm, x_own, load_sem.at[0]),
        pltpu.make_async_copy(qw_hbm, w_all.at[:, pl.ds(0, 2 * HD)], load_sem.at[1]),
        pltpu.make_async_copy(kw_hbm, w_all.at[:, pl.ds(2 * HD, HD)], load_sem.at[2]),
        pltpu.make_async_copy(vw_hbm, w_all.at[:, pl.ds(3 * HD, HD)], load_sem.at[3]),
        pltpu.make_async_copy(o_hbm.at[:, own_cols], o_all.at[0], load_sem.at[4]),
    ]
    for load in loads:
        load.start()

    lens = [lens_ref[me, s] for s in range(slots)]
    dests = [dest_ref[me, s] for s in range(slots)]
    row = lax.broadcasted_iota(jnp.int32, (1, home), 1)
    col = lax.broadcasted_iota(jnp.int32, (home, 1), 0)
    to_send = jnp.full((1, home), -1, jnp.int32)
    to_work = jnp.full((1, home), -1, jnp.int32)
    start = jnp.zeros((home, 1), jnp.int32)
    offset = jnp.int32(0)
    staying = jnp.int32(0)
    for s in range(slots):
        before = jnp.int32(0)
        for t in range(s):
            before = before + jnp.where(dests[t] == dests[s], lens[t], 0)
        shift = dests[s] - me
        shift = jnp.where(shift < 0, shift + replicas, shift)
        stays = shift == 0
        send_base = jnp.where(stays, -home, shift * CAPP + before - offset)
        work_base = jnp.where(stays, before - offset, -2 * home)
        to_send = jnp.where(row >= offset, row + send_base - jnp.where(stays, home, 0), to_send)
        to_work = jnp.where(row >= offset, row + work_base, to_work)
        start = jnp.where(col >= offset, offset, start)
        staying = staying + jnp.where(stays, lens[s], 0)
        offset = offset + lens[s]
    to_send = jnp.where(row >= offset, -1, to_send)
    to_work = jnp.where(row >= offset, -1, to_work)
    pool = replicas * CAPP
    send_hot = one_hot(lax.broadcasted_iota(jnp.int32, (pool, home), 0) == to_send)

    x_recv[pl.ds(0, CAPP), :] = jnp.zeros((CAPP, half), BF16)
    h_recv[pl.ds(0, CAPP), :] = jnp.zeros((CAPP, h_recv.shape[1]), BF16)

    loads[0].wait()

    @pl.loop(0, chunks)
    def _(c):
        cols = pl.ds(pl.multiple_of(c * CHUNK, CHUNK), CHUNK)
        x_send[:, cols] = dot(send_hot, x_own[:, cols]).astype(BF16)

    def square_sum(x_ref):
        def step(c, total):
            for piece in range(CHUNK // 128):
                cols = pl.ds(pl.multiple_of(c * CHUNK + piece * 128, 128), 128)
                wide = x_ref[:, cols].astype(F32)
                total = total + wide * wide
            return total

        return lax.fori_loop(0, chunks, step, jnp.zeros((home, 128), F32))

    pl.semaphore_wait(barrier, replicas)


    pair_x = pltpu.make_async_remote_copy(
        x_own, x_other, pair_send.at[0], pair_recv.at[0], {"tensor": 1 - part}, MESH
    )
    pair_x.start()

    def exchange(source, target, send_sem, recv_sem):
        copies = []
        for k in range(1, replicas):
            copies.append(
                pltpu.make_async_remote_copy(
                    source.at[pl.ds(k * CAPP, CAPP)],
                    target.at[pl.ds((replicas - k) * CAPP, CAPP)],
                    send_sem.at[k],
                    recv_sem.at[replicas - k],
                    {"dp": peers[k]},
                    MESH,
                )
            )
        for copy in copies:
            copy.start()
        return copies

    x_first = exchange(x_send.at[:, early], x_recv.at[:, early], xs_sem.at[0], xr_sem.at[0])
    squares_own[...] = square_sum(x_own)
    pair_s = pltpu.make_async_remote_copy(
        squares_own, squares_other, pair_send.at[3], pair_recv.at[3], {"tensor": 1 - part}, MESH
    )
    pair_s.start()
    pair_o = pltpu.make_async_remote_copy(
        o_hbm.at[:, other_cols], o_all.at[1], pair_send.at[1], pair_recv.at[1], {"tensor": 1 - part}, MESH
    )

    slot = lax.broadcasted_iota(jnp.int32, (1, pool), 1)
    from_pool = jnp.full((1, pool), -1, jnp.int32)
    begin = staying
    for k in range(1, replicas):
        count = jnp.int32(0)
        for s in range(slots):
            count = count + jnp.where(dest_ref[peers[k], s] == me, lens_ref[peers[k], s], 0)
        inside = (slot >= k * CAPP) & (slot < k * CAPP + count)
        from_pool = jnp.where(inside, slot + (begin - k * CAPP), from_pool)
        begin = begin + count
    home_hot = one_hot(lax.broadcasted_iota(jnp.int32, (work, home), 0) == to_work)
    pool_hot = one_hot(lax.broadcasted_iota(jnp.int32, (work, pool), 0) == from_pool)

    angles = (col - start).astype(F32) * rope_ref[0:1, :]
    cosine = jnp.cos(angles)
    sine = jnp.sin(angles) * rope_ref[1:2, :]

    for load in loads[1:4]:
        load.wait()
    pair_s.wait_recv()
    squares = squares_own[...] + squares_other[...]
    scale = lax.rsqrt(jnp.sum(squares, axis=1, keepdims=True) / (2 * half) + EPSILON)

    def project(x_ref, base, step):
        cols = pl.ds(step * WIDE, WIDE)
        rows = pl.ds(pl.multiple_of(base + step * WIDE, WIDE), WIDE)
        normed = (x_ref[:, cols].astype(F32) * scale * gain_ref[:, rows]).astype(BF16)
        return dot(normed, w_all[rows, :])

    qkv[...] = project(x_own, part * half, 0)
    for step in range(1, half // WIDE):
        qkv[...] += project(x_own, part * half, step)
    pair_x.wait_recv()
    pair_o.start()
    for step in range(half // WIDE):
        qkv[...] += project(x_other, (1 - part) * half, step)

    def rotated(entries, gain):
        entries = head_norm(entries, gain)
        return (entries * cosine + pltpu.roll(entries, HD // 2, 1) * sine).astype(BF16)

    keys = rotated(qkv[:, pl.ds(2 * HD, HD)], k_gain_ref[...])
    values = qkv[:, pl.ds(3 * HD, HD)].astype(BF16)
    key_id = lax.broadcasted_iota(jnp.int32, (home, home), 1)
    query_id = lax.broadcasted_iota(jnp.int32, (home, home), 0)
    allowed = (key_id >= start) & (key_id <= query_id)
    for h in range(2):
        queries = rotated(qkv[:, pl.ds(h * HD, HD)], q_gain_ref[...])
        scores = lax.dot_general(
            queries, keys, (((1,), (1,)), ((), ())), preferred_element_type=F32
        ) * HD ** (-0.5)
        scores = jnp.where(allowed, scores, MASKED_SCORE)
        exp_scores = jnp.exp(scores - jnp.max(scores, axis=1, keepdims=True))
        weights = (exp_scores / jnp.sum(exp_scores, axis=1, keepdims=True)).astype(BF16)
        h_own[:, pl.ds(h * HD, HD)] = dot(weights, values).astype(BF16)

    h_send[...] = dot(send_hot, h_own[...]).astype(BF16)
    h_copies = exchange(h_send, h_recv, hs_sem, hr_sem)
    x_last = exchange(x_send.at[:, late], x_recv.at[:, late], xs_sem.at[1], xr_sem.at[1])
    pair_h = pltpu.make_async_remote_copy(
        h_own, h_other, pair_send.at[2], pair_recv.at[2], {"tensor": 1 - part}, MESH
    )
    pair_h.start()
    loads[4].wait()
    home_own = dot(home_hot, h_own[...]).astype(BF16)
    pair_h.wait_recv()
    home_other = dot(home_hot, h_other[...]).astype(BF16)
    pair_o.wait_recv()

    @pl.loop(0, chunks)
    def _(c):
        cols = pl.ds(pl.multiple_of(c * CHUNK, CHUNK), CHUNK)
        attended = dot(home_own, o_all[0, :, cols]) + dot(home_other, o_all[1, :, cols])
        result[:, cols] = dot(home_hot, x_own[:, cols]) + attended

    for copy in h_copies:
        copy.wait_recv()
    pair_r = pltpu.make_async_remote_copy(
        h_recv, h_pass, pair_send.at[4], pair_recv.at[4], {"tensor": 1 - part}, MESH
    )
    pair_r.start()
    pool_own = dot(pool_hot, h_recv[...]).astype(BF16)

    @pl.loop(0, chunks)
    def _(c):
        cols = pl.ds(pl.multiple_of(c * CHUNK, CHUNK), CHUNK)
        result[:, cols] += dot(pool_own, o_all[0, :, cols])

    pair_r.wait_recv()
    pool_other = dot(pool_hot, h_pass[...]).astype(BF16)

    @pl.loop(0, chunks)
    def _(c):
        cols = pl.ds(pl.multiple_of(c * CHUNK, CHUNK), CHUNK)
        result[:, cols] += dot(pool_other, o_all[1, :, cols])

    writes = []
    for c in range(chunks):
        if c in (0, ahead):
            for copy in x_first if c == 0 else x_last:
                copy.wait_recv()
        cols = pl.ds(c * CHUNK, CHUNK)
        out_buf[:, cols] = (result[:, cols] + dot(pool_hot, x_recv[:, cols])).astype(BF16)
        write = pltpu.make_async_copy(out_buf.at[:, cols], out_hbm.at[:, cols], out_sem.at[c])
        write.start()
        writes.append(write)
    for copy in [pair_s, pair_x, pair_o, pair_h, pair_r] + x_first + x_last + h_copies:
        copy.wait_send()
    for write in writes:
        write.wait()


def per_device(
    hidden_states,
    input_gain,
    q_weight,
    k_weight,
    v_weight,
    o_weight,
    q_gain,
    k_gain,
    seq_lens,
    dest,
):
    replicas = lax.axis_size("dp")
    home, half = hidden_states.shape
    slots = seq_lens.shape[1]
    work = max(LONG, slots * SHORT + (slots - 1) * CAPP)
    pool = replicas * CAPP
    width = o_weight.shape[0]
    channel = np.arange(HD)
    frequency = ROPE_BASE ** (-2.0 * (channel % (HD // 2)) / HD)
    sign = np.where(channel < HD // 2, -1.0, 1.0)
    rope = jnp.asarray(np.stack([frequency, sign]).astype(np.float32))
    vmem = pl.BlockSpec(memory_space=pltpu.VMEM)
    smem = pl.BlockSpec(memory_space=pltpu.SMEM)
    hbm = pl.BlockSpec(memory_space=pl.ANY)
    dma = pltpu.SemaphoreType.DMA
    return pl.pallas_call(
        functools.partial(kernel, replicas),
        out_shape=jax.ShapeDtypeStruct((work, half), BF16),
        in_specs=[smem, smem, vmem, vmem, vmem, vmem] + [hbm] * 5,
        out_specs=hbm,
        scratch_shapes=[
            pltpu.VMEM((home, half), BF16),
            pltpu.VMEM((home, half), BF16),
            pltpu.VMEM((2 * half, 4 * HD), BF16),
            pltpu.VMEM((2, width, half), BF16),
            pltpu.VMEM((pool, half), BF16),
            pltpu.VMEM((pool, half), BF16),
            pltpu.VMEM((home, width), BF16),
            pltpu.VMEM((home, width), BF16),
            pltpu.VMEM((pool, width), BF16),
            pltpu.VMEM((pool, width), BF16),
            pltpu.VMEM((pool, width), BF16),
            pltpu.VMEM((home, 128), F32),
            pltpu.VMEM((home, 128), F32),
            pltpu.VMEM((home, 4 * HD), F32),
            pltpu.VMEM((work, half), F32),
            pltpu.VMEM((work, half), BF16),
            dma((5,)),
            dma((5,)),
            dma((5,)),
            dma((2, replicas)),
            dma((2, replicas)),
            dma((replicas,)),
            dma((replicas,)),
            dma((half // CHUNK,)),
        ],
        compiler_params=pltpu.CompilerParams(
            collective_id=0,
            has_side_effects=True,
            vmem_limit_bytes=56 * 1024 * 1024,
        ),
    )(
        seq_lens,
        dest,
        rope,
        q_gain.reshape(1, HD),
        k_gain.reshape(1, HD),
        input_gain.reshape(1, -1),
        hidden_states,
        q_weight,
        k_weight,
        v_weight,
        o_weight,
    )


def solution(mesh):
    return jax.shard_map(
        per_device,
        mesh=mesh,
        in_specs=(
            P(("groups", "dp"), "tensor"),
            P(),
            P(None, "tensor"),
            P(None, "tensor"),
            P(None, "tensor"),
            P("tensor", None),
            P(),
            P(),
            P("groups", None),
            P("groups", None),
        ),
        out_specs=P(("groups", "dp"), "tensor"),
        check_vma=False,
    )
```
